512 devices in a mesh: dom: 128 (over z, y, x_lo), edge: 4 (over x_hi, core).
Axes of the slice: x: 4 (x_hi: 2, x_lo: 2; x = x_hi * 2 + x_lo), y: 4, z: 16, core: 2. Of those that a mesh axis runs over, the one named last changes fastest.
Arguments:
- embeddings: float32 [65536, 400], P(('dom', 'edge')), may hold values from -1.2 to 1.2
- adagrad_state: float32 [65536], P(('dom', 'edge')), may hold values from 0.01 to 1
- relations: bfloat16 [256, 400], replicated, may hold values from -4 to 4
- endpoints: int32 [2, 2, 128, 2048], P(None, None, 'dom', 'edge'), may hold values from 0 to 511
- relation_ids: int32 [2, 128, 2048], P(None, 'dom', 'edge'), may hold values from 0 to 255
- negatives: int32 [2, 2, 128, 8, 256], P(None, None, 'dom', 'edge'), may hold values from 0 to 511
- edge_counts: int32 [2, 128, 4], P(None, 'dom', 'edge'), may hold values from 1 to 512, as said below
- plan: int32 [2], replicated, may hold values from 1 to 127, as said below
Outputs:
- new_embeddings: float32 [65536, 400], P(('dom', 'edge'))
- new_state: float32 [65536], P(('dom', 'edge'))
The draws below stay inside these ranges and needn't reach their ends.
Inputs may be any that keep to these rules, and one draw needn't show every extreme that they name: `edge_counts`: in every round some edge group has all 512 slots live; live slots come first. `plan`: consecutive rounds have different patterns; some round has the pattern 128 - 1.
All inputs are finite; a program needn't handle non-finite values.
Results may differ from the reference program's by a relative error of at most 0.01.
Values may be sent and summed in bfloat16 or wider, within the bound.
A program may use at most 64 MiB of HBM per device.

```python
import math
import jax
import jax.numpy as jnp
import numpy as np
from jax import lax

D = 400
REL = 256
EDGE_DEV = 512
BLOCK = 256
NEG = 256
ROUNDS = 2
PARTITIONS = 128
EDGE_GROUPS = 4
PART_ROWS = 512
ENTITIES = 65536
EDGE_SLOTS = 2048
BLOCK_SLOTS = 8


def draw_edge_counts(key, part):
    key_first, key_second, key_full = jax.random.split(jax.random.fold_in(key, 71), 3)
    shape = (ROUNDS, PARTITIONS, EDGE_GROUPS)
    first_draw = jax.random.randint(key_first, shape, 0, EDGE_DEV)
    second_draw = jax.random.randint(key_second, shape, 0, EDGE_DEV)
    counts = EDGE_DEV - first_draw * second_draw // (4 * EDGE_DEV)
    flattened = counts.reshape(ROUNDS, PARTITIONS * EDGE_GROUPS)
    chosen = jax.random.randint(key_full, (ROUNDS,), 0, PARTITIONS * EDGE_GROUPS)
    places = jnp.arange(PARTITIONS * EDGE_GROUPS, dtype=jnp.int32)
    flattened = jnp.where(places[None, :] == chosen[:, None], EDGE_DEV, flattened)
    return flattened.reshape(shape).astype(jnp.int32)


def draw_plan(key, part):
    key_start, key_steps, key_top = jax.random.split(jax.random.fold_in(key, 93), 3)
    start = jax.random.randint(key_start, (1,), 0, PARTITIONS - 2)
    steps = jax.random.randint(key_steps, (ROUNDS,), 1, PARTITIONS - 2)
    places = jnp.arange(ROUNDS, dtype=jnp.int32)
    steps = jnp.where(places == 0, 0, steps)
    offsets = jnp.cumsum(steps) + start
    walked = offsets % (PARTITIONS - 2) + 1
    top_round = jax.random.randint(key_top, (1,), 0, ROUNDS)
    return jnp.where(places == top_round, PARTITIONS - 1, walked).astype(jnp.int32)


def plant(result, rng, smallest, largest):
    dims = result.shape
    place = [jax.random.randint(jax.random.fold_in(rng, axis), (), 0, dims[axis]) for axis in range(len(dims))]
    result = result.at[tuple(place)].set(smallest)
    longest = dims.index(max(dims))
    place[longest] = (place[longest] + 1) % dims[longest]
    return result.at[tuple(place)].set(largest)


def block_scale(stream_key, dims, shards, smallest, top_value):
    factor_of, own = 1.0, jax.random.fold_in(stream_key, 6)
    for dim, blocks in shards:
        steps = jnp.exp(jax.random.uniform(jax.random.fold_in(own, dim), (blocks,), jnp.float32, smallest / len(shards), top_value / len(shards)))
        factor_of = factor_of * jnp.repeat(steps, dims[dim] // blocks).reshape([-1 if axis == dim else 1 for axis in range(len(dims))])
    return factor_of


def cumulative_ranks(number_of, skew):
    portions = [(1 << 20) // math.isqrt(standing ** skew) + 1 for standing in range(1, number_of + 1)]
    deviation = 1 + sum(portions) // (1 << 30)
    return np.cumsum(np.array([max(1, weight // deviation) for weight in portions]))


def ranked_ids(own_key, shape, count, skew):
    table = cumulative_ranks(count, skew)
    lot = jax.random.randint(jax.random.fold_in(own_key, 1), shape, 0, int(table[count - 1]))
    rank = jnp.searchsorted(jnp.asarray(table, jnp.int32), lot, side="right")
    return jax.random.permutation(jax.random.fold_in(own_key, 2), count)[rank].astype(jnp.int32)


def centred(own_key, dims, width, bound, pieces=(), kind=jnp.bfloat16):
    factor_of = block_scale(own_key, dims, pieces, -0.22, 0.18) if pieces else 1.0
    entries = jax.random.normal(own_key, dims, jnp.float32) * width * factor_of
    return jnp.minimum(jnp.maximum(entries, -bound), bound).astype(kind)


def setup_inputs(seed: int = 0) -> dict:
    splits = jax.random.split(jax.random.key(seed), 9)
    return {
        "embeddings": centred(splits[0], (ENTITIES, D), 0.2, 1.2, ((0, 512),), jnp.float32),
        "adagrad_state": jnp.clip(jnp.exp(math.log(1.0) - 4.6051702 * jax.random.uniform(splits[1], (ENTITIES,), jnp.float32) ** block_scale(splits[1], (ENTITIES,), ((0, 512),), -0.2, 0.2)), 0.01, 1.0),
        "relations": centred(splits[2], (REL, D), 1.0, 4.0),
        "endpoints": plant(jax.random.randint(splits[3], (ROUNDS, 2, PARTITIONS, EDGE_SLOTS), 0, PART_ROWS), jax.random.fold_in(splits[3], 1), 0, PART_ROWS - 1).astype(jnp.int32),
        "relation_ids": plant(ranked_ids(splits[4], (ROUNDS, PARTITIONS, EDGE_SLOTS), REL, 2), jax.random.fold_in(splits[4], 3), 0, REL - 1).astype(jnp.int32),
        "negatives": plant(jax.random.randint(splits[5], (ROUNDS, 2, PARTITIONS, BLOCK_SLOTS, NEG), 0, PART_ROWS), jax.random.fold_in(splits[5], 1), 0, PART_ROWS - 1).astype(jnp.int32),
        "edge_counts": draw_edge_counts(jax.random.fold_in(splits[8], 71), 0),
        "plan": draw_plan(jax.random.fold_in(splits[8], 71), 0),
    }


learning_rate = 0.2

def round_trip(values):
    return lax.optimization_barrier(values.astype(jnp.bfloat16)).astype(jnp.float32)

def complex_product(left, right):
    half = left.shape[-1] // 2
    left_real, left_imag = (left[..., :half], left[..., half:])
    right_real, right_imag = (right[..., :half], right[..., half:])
    return jnp.concatenate([left_real * right_real - left_imag * right_imag, left_real * right_imag + left_imag * right_real], axis=-1)

def conjugate(values):
    half = values.shape[-1] // 2
    return jnp.concatenate([values[..., :half], -values[..., half:]], axis=-1)

def group_terms(own, other, rel_table, lhs_ids, rhs_ids, rel_ids, neg_lhs, neg_rhs, count):
    blocks = neg_lhs.shape[0]
    lhs = own[lhs_ids]
    rhs = other[rhs_ids]
    rel = rel_table[rel_ids]
    queries = round_trip(complex_product(lhs, rel))
    backs = round_trip(complex_product(conjugate(rel), rhs))
    positive = lax.optimization_barrier(jnp.sum(queries * rhs, axis=-1))
    neg_rhs_rows = other[neg_rhs]
    neg_lhs_rows = own[neg_lhs]
    hp = lax.Precision.HIGHEST
    query_blocks = queries.reshape(blocks, BLOCK, D)
    back_blocks = backs.reshape(blocks, BLOCK, D)
    scores_rhs = jnp.einsum('cqd,cnd->cqn', query_blocks, neg_rhs_rows, precision=hp)
    scores_lhs = jnp.einsum('cqd,cnd->cqn', back_blocks, neg_lhs_rows, precision=hp)
    live = (jnp.arange(EDGE_DEV, dtype=jnp.int32) < count).astype(jnp.float32)
    live_blocks = live.reshape(blocks, BLOCK, 1)
    weight_pos = -jax.nn.sigmoid(-positive) * live
    weight_rhs = round_trip(jax.nn.sigmoid(scores_rhs) * live_blocks * (0.5 / NEG))
    weight_lhs = round_trip(jax.nn.sigmoid(scores_lhs) * live_blocks * (0.5 / NEG))
    grad_query = weight_pos[:, None] * rhs + jnp.einsum('cqn,cnd->cqd', weight_rhs, neg_rhs_rows, precision=hp).reshape(EDGE_DEV, D)
    grad_back = jnp.einsum('cqn,cnd->cqd', weight_lhs, neg_lhs_rows, precision=hp).reshape(EDGE_DEV, D)
    grad_lhs = round_trip(complex_product(grad_query, conjugate(rel)))
    grad_rhs = round_trip(weight_pos[:, None] * queries + complex_product(grad_back, rel))
    grad_neg_rhs = round_trip(jnp.einsum('cqn,cqd->cnd', weight_rhs, query_blocks, precision=hp)).reshape(-1, D)
    grad_neg_lhs = round_trip(jnp.einsum('cqn,cqd->cnd', weight_lhs, back_blocks, precision=hp)).reshape(-1, D)
    own_part = jax.ops.segment_sum(grad_lhs, lhs_ids, num_segments=PART_ROWS) + jax.ops.segment_sum(grad_neg_lhs, neg_lhs.reshape(-1), num_segments=PART_ROWS)
    other_part = jax.ops.segment_sum(grad_rhs, rhs_ids, num_segments=PART_ROWS) + jax.ops.segment_sum(grad_neg_rhs, neg_rhs.reshape(-1), num_segments=PART_ROWS)
    return (own_part, other_part)

def reference(embeddings, adagrad_state, relations, endpoints, relation_ids, negatives, edge_counts, plan):
    blocks_dev = EDGE_DEV // BLOCK
    rel_table = relations.astype(jnp.float32)
    table = embeddings.reshape(PARTITIONS, PART_ROWS, D)
    state = adagrad_state.reshape(PARTITIONS, PART_ROWS)
    for round_index in range(ROUNDS):
        partner_ids = jnp.bitwise_xor(jnp.arange(PARTITIONS, dtype=jnp.int32), plan[round_index])
        rounded = round_trip(table)

        def bucket(partition):
            own = rounded[partition]
            other = rounded[partner_ids[partition]]
            grads_own = jnp.zeros((PART_ROWS, D), jnp.float32)
            grads_other = jnp.zeros((PART_ROWS, D), jnp.float32)
            for group_index in range(EDGE_GROUPS):
                start = group_index * EDGE_DEV
                first = group_index * blocks_dev
                own_part, other_part = group_terms(own, other, rel_table, endpoints[round_index, 0, partition, start:start + EDGE_DEV], endpoints[round_index, 1, partition, start:start + EDGE_DEV], relation_ids[round_index, partition, start:start + EDGE_DEV], negatives[round_index, 0, partition, first:first + blocks_dev], negatives[round_index, 1, partition, first:first + blocks_dev], edge_counts[round_index, partition, group_index])
                grads_own = grads_own + round_trip(own_part)
                grads_other = grads_other + round_trip(other_part)
            return (grads_own, grads_other)
        grads_lhs, grads_rhs = lax.map(bucket, jnp.arange(PARTITIONS, dtype=jnp.int32))
        returned = round_trip(grads_rhs)[partner_ids]
        total = grads_lhs + returned
        state = state + lax.optimization_barrier(jnp.mean(total * total, axis=-1))
        table = table - learning_rate * total / jnp.sqrt(state)[..., None]
    return (table.reshape(ENTITIES, D), state.reshape(ENTITIES))
```

```python
import jax
import jax.numpy as jnp
from jax import lax
from jax.sharding import PartitionSpec as P

learning_rate = 0.2


def in_one_piece(arrays, axis, dim, along):
    both = jnp.concatenate(arrays, axis=along)
    filled, at, gathered = (lax.all_gather(both, axis, axis=dim, tiled=True), 0, [])
    for a in arrays:
        gathered.append(lax.slice_in_dim(filled, at, at + a.shape[along], axis=along))
        at += a.shape[along]
    return tuple(gathered)


def split_up(shard, dim, size):
    before, after = (shard.shape[:dim], shard.shape[dim + 1 :])
    return jnp.moveaxis(shard.reshape(*before, size, -1, *after), dim, 0)


def sent_and_summed(shard, axis, dim):
    tiles = split_up(shard, dim, lax.axis_size(axis))
    arrived = lax.all_to_all(tiles, axis, split_axis=0, concat_axis=0, tiled=True)
    return arrived.astype(jnp.float32).sum(axis=0)


def in_one_piece_2(arrays, axis, dim, along):
    both = jnp.concatenate(arrays, axis=along)
    filled, at, gathered = (sent_and_summed(both, axis, dim), 0, [])
    for a in arrays:
        gathered.append(lax.slice_in_dim(filled, at, at + a.shape[along], axis=along))
        at += a.shape[along]
    return tuple(gathered)


def complex_product(left, right):
    half = left.shape[-1] // 2
    left_real, left_imag = (left[..., :half], left[..., half:])
    right_real, right_imag = (right[..., :half], right[..., half:])
    return jnp.concatenate(
        [
            left_real * right_real - left_imag * right_imag,
            left_real * right_imag + left_imag * right_real,
        ],
        axis=-1,
    )


def conjugate(values):
    half = values.shape[-1] // 2
    return jnp.concatenate([values[..., :half], -values[..., half:]], axis=-1)


def exchange(values, mask_value):
    size = lax.axis_size("dom")

    def branch(mask):
        pairs = [(source, source ^ mask) for source in range(size)]
        return lambda v: lax.ppermute(v, "dom", pairs)

    return lax.switch(mask_value - 1, [branch(mask) for mask in range(1, size)], values)


def onehot_rows(indices, count):
    return (indices[:, None] == jnp.arange(count, dtype=jnp.int32)[None, :]).astype(jnp.bfloat16)


def transposed_product(onehot, values):
    return lax.dot_general(
        onehot, values, (((0,), (0,)), ((), ())), preferred_element_type=jnp.float32
    )


def bucket_terms(
    full_own, full_partner, relations, lhs_ids, rhs_ids, rel_ids, neg_lhs, neg_rhs, count
):
    part_rows, width = full_own.shape
    edge_slots = lhs_ids.shape[0]
    blocks, negs = neg_lhs.shape
    block_rows = edge_slots // blocks
    onehot_lhs = onehot_rows(lhs_ids, part_rows)
    onehot_rhs = onehot_rows(rhs_ids, part_rows)
    onehot_neg_lhs = onehot_rows(neg_lhs.reshape(-1), part_rows)
    onehot_neg_rhs = onehot_rows(neg_rhs.reshape(-1), part_rows)
    onehot_rel = onehot_rows(rel_ids, relations.shape[0])
    lhs = jnp.dot(onehot_lhs, full_own, preferred_element_type=jnp.float32)
    rhs = jnp.dot(onehot_rhs, full_partner, preferred_element_type=jnp.float32)
    rel = jnp.dot(onehot_rel, relations, preferred_element_type=jnp.float32)
    neg_lhs_rows = (
        jnp.dot(onehot_neg_lhs, full_own, preferred_element_type=jnp.float32)
        .astype(jnp.bfloat16)
        .reshape(blocks, negs, width)
    )
    neg_rhs_rows = (
        jnp.dot(onehot_neg_rhs, full_partner, preferred_element_type=jnp.float32)
        .astype(jnp.bfloat16)
        .reshape(blocks, negs, width)
    )
    queries = complex_product(lhs, rel).astype(jnp.bfloat16)
    backs = complex_product(conjugate(rel), rhs).astype(jnp.bfloat16)
    query_float = queries.astype(jnp.float32)
    positive = jnp.sum(query_float * rhs, axis=-1)
    query_blocks = queries.reshape(blocks, block_rows, width)
    back_blocks = backs.reshape(blocks, block_rows, width)
    scores_rhs = jnp.einsum(
        "cqd,cnd->cqn", query_blocks, neg_rhs_rows, preferred_element_type=jnp.float32
    )
    scores_lhs = jnp.einsum(
        "cqd,cnd->cqn", back_blocks, neg_lhs_rows, preferred_element_type=jnp.float32
    )
    live = (jnp.arange(edge_slots, dtype=jnp.int32) < count).astype(jnp.float32)
    live_blocks = live.reshape(blocks, block_rows, 1)
    weight_pos = -jax.nn.sigmoid(-positive) * live
    weight_rhs = (jax.nn.sigmoid(scores_rhs) * live_blocks * (0.5 / negs)).astype(jnp.bfloat16)
    weight_lhs = (jax.nn.sigmoid(scores_lhs) * live_blocks * (0.5 / negs)).astype(jnp.bfloat16)
    grad_query = weight_pos[:, None] * rhs + jnp.einsum(
        "cqn,cnd->cqd", weight_rhs, neg_rhs_rows, preferred_element_type=jnp.float32
    ).reshape(edge_slots, width)
    grad_back = jnp.einsum(
        "cqn,cnd->cqd", weight_lhs, neg_lhs_rows, preferred_element_type=jnp.float32
    ).reshape(edge_slots, width)
    grad_lhs = complex_product(grad_query, conjugate(rel)).astype(jnp.bfloat16)
    grad_rhs = (weight_pos[:, None] * query_float + complex_product(grad_back, rel)).astype(
        jnp.bfloat16
    )
    grad_neg_rhs = (
        jnp.einsum("cqn,cqd->cnd", weight_rhs, query_blocks, preferred_element_type=jnp.float32)
        .astype(jnp.bfloat16)
        .reshape(-1, width)
    )
    grad_neg_lhs = (
        jnp.einsum("cqn,cqd->cnd", weight_lhs, back_blocks, preferred_element_type=jnp.float32)
        .astype(jnp.bfloat16)
        .reshape(-1, width)
    )
    own_part = transposed_product(onehot_lhs, grad_lhs) + transposed_product(
        onehot_neg_lhs, grad_neg_lhs
    )
    other_part = transposed_product(onehot_rhs, grad_rhs) + transposed_product(
        onehot_neg_rhs, grad_neg_rhs
    )
    return (own_part, other_part)


def on_device(
    embeddings, adagrad_state, relations, endpoints, relation_ids, negatives, edge_counts, plan
):
    table = embeddings
    state = adagrad_state
    for round_index in range(plan.shape[0]):
        mask_value = plan[round_index]
        own_rounded = table.astype(jnp.bfloat16)
        partner_rounded = exchange(own_rounded, mask_value)
        full_own, full_partner = in_one_piece((own_rounded, partner_rounded), "edge", 0, 1)
        own_part, other_part = bucket_terms(
            full_own,
            full_partner,
            relations,
            endpoints[round_index, 0, 0],
            endpoints[round_index, 1, 0],
            relation_ids[round_index, 0],
            negatives[round_index, 0, 0],
            negatives[round_index, 1, 0],
            edge_counts[round_index, 0, 0],
        )
        own_share, other_share = in_one_piece_2(
            (own_part.astype(jnp.bfloat16), other_part.astype(jnp.bfloat16)), "edge", 0, 1
        )
        returned = exchange(other_share.astype(jnp.bfloat16), mask_value).astype(
            jnp.float32
        )
        total = own_share + returned
        state = state + jnp.mean(total * total, axis=1)
        table = table - learning_rate * total / jnp.sqrt(state)[:, None]
    return (table, state)


def solution(mesh):
    in_specs = (
        P(("dom", "edge"), None),
        P(("dom", "edge")),
        P(),
        P(None, None, "dom", "edge"),
        P(None, "dom", "edge"),
        P(None, None, "dom", "edge", None),
        P(None, "dom", "edge"),
        P(),
    )
    out_specs = (P(("dom", "edge"), None), P(("dom", "edge")))
    return jax.shard_map(
        on_device, mesh=mesh, in_specs=in_specs, out_specs=out_specs, check_vma=False
    )
```

```python
import functools

import jax
import jax.numpy as jnp
from jax import lax
from jax.experimental import pallas as pl
from jax.experimental.pallas import tpu as pltpu
from jax.sharding import PartitionSpec as P

MESH = pl.DeviceIdType.MESH
learning_rate = 0.2
LANES = 128
LOW_BITS = 3
IDX_ROWS = 16


def xor(value, mask):
    out = value
    for bit in range(mask.bit_length()):
        if mask >> bit & 1:
            out = out + (1 << bit) * (1 - 2 * (value // (1 << bit) % 2))
    return out


def columns(index):
    return pl.ds(pl.multiple_of(index * LANES, LANES), LANES)


def greet(devices):
    barrier = pltpu.get_barrier_semaphore()
    for device in devices:
        pl.semaphore_signal(barrier, inc=1, device_id=device, device_id_type=MESH)


def greeted(count):
    pl.semaphore_wait(pltpu.get_barrier_semaphore(), count)


def far_kernel(mask, mine, idx, own_full, other, other_idx, send, recv, local):
    dom, edge = lax.axis_index("dom"), lax.axis_index("edge")
    mates = [(dom, (edge + k) % 4) for k in range(1, 4)]
    across = (xor(dom, mask << LOW_BITS), edge)
    greet(mates + ([across] if mask else []))
    greeted(4 if mask else 3)
    copies = []
    if mask:
        for at, (src, dst) in enumerate(((mine, other), (idx, other_idx))):
            copies.append(
                pltpu.make_async_remote_copy(
                    src, dst, send.at[at], recv.at[at], device_id=across, device_id_type=MESH
                )
            )
    for k, mate in enumerate(mates):
        copies.append(
            pltpu.make_async_remote_copy(
                mine,
                own_full.at[:, columns(edge)],
                send.at[2 + k],
                recv.at[2 + k],
                device_id=mate,
                device_id_type=MESH,
            )
        )
    kept = pltpu.make_async_copy(mine, own_full.at[:, columns(edge)], local.at[0])
    for copy in copies:
        copy.start()
    kept.start()
    if not mask:
        other[...] = mine[...]
        other_idx[...] = idx[...]
    kept.wait()
    for copy in copies:
        copy.wait()


def near_kernel(mask, shard, idx, full, full_idx, send, recv, local):
    dom, edge = lax.axis_index("dom"), lax.axis_index("edge")
    chip, core = edge // 2, edge % 2
    partner = xor(dom, mask)
    sibling = (dom, chip * 2 + (1 - core))
    other_chip = (dom, (1 - chip) * 2 + core)
    targets = [(partner, edge), (partner, (1 - chip) * 2 + core)]
    if mask:
        greet([sibling] + targets)
        greeted(3)
    else:
        greet([sibling, other_chip])
        greeted(2)
    here, there = columns(edge), columns((1 - chip) * 2 + core)
    straight = crossed = moved = None
    crossed = pltpu.make_async_remote_copy(
        shard, full.at[:, here], send.at[1], recv.at[1], device_id=targets[1], device_id_type=MESH
    )
    crossed.start()
    if mask:
        straight = pltpu.make_async_remote_copy(
            shard, full.at[:, here], send.at[0], recv.at[0], device_id=targets[0], device_id_type=MESH
        )
        moved = pltpu.make_async_remote_copy(
            idx, full_idx, send.at[2], recv.at[2], device_id=targets[0], device_id_type=MESH
        )
        straight.start()
        moved.start()
    else:
        kept = pltpu.make_async_copy(shard, full.at[:, here], local.at[0])
        kept.start()
        full_idx[...] = idx[...]
        kept.wait()
    if mask:
        straight.wait_recv()
    first = pltpu.make_async_remote_copy(
        full.at[:, here],
        full.at[:, here],
        send.at[3],
        recv.at[3],
        device_id=sibling,
        device_id_type=MESH,
    )
    first.start()
    crossed.wait_recv()
    second = pltpu.make_async_remote_copy(
        full.at[:, there],
        full.at[:, there],
        send.at[4],
        recv.at[4],
        device_id=sibling,
        device_id_type=MESH,
    )
    second.start()
    crossed.wait_send()
    if mask:
        straight.wait_send()
        moved.wait()
    first.wait()
    second.wait()


def across_rows(left, right):
    return lax.dot_general(left, right, (((1,), (1,)), ((), ())), preferred_element_type=jnp.float32)


def product(left, right):
    return jnp.dot(left, right, preferred_element_type=jnp.float32)


def halves(values):
    half = values.shape[0] // 2
    return values[:half], values[half:]


def ones_where(condition):
    return jnp.where(condition, 1.0, 0.0)


def round_kernel(
    own, other, idx, other_idx, relations, table, state,
    table_out, state_out, shard_out,
    own_rows, other_rows, total, parts, arrived, send, recv,
):
    dom, edge = lax.axis_index("dom"), lax.axis_index("edge")
    mates = [(dom, (edge + k) % 4) for k in range(1, 4)]
    greet(mates)
    rows = own.shape[1]
    width = own.shape[0]
    block = 2 * LANES
    own_rows[...] = own[...].T
    other_rows[...] = other[...].T
    total[...] = jnp.zeros_like(total)

    def packed(group, base, at):
        def row(ref, i):
            return ref[pl.ds(base + at + i, 1), :]

        both = [
            jnp.where(group == 0, row(idx, i), row(other_idx, i)) for i in range(2)
        ]
        both = jnp.concatenate(both, axis=1)
        return both & 65535, both >> 16

    def step(b, carry):
        group, at = b // 2, b % 2 * 2
        own_ids, other_ids = packed(group, 0, at)
        rel_ids, count = packed(group, 4, at)
        own_neg, other_neg = packed(group, 8, at)
        row_of = lax.broadcasted_iota(jnp.int32, (rows, block), 0)
        slot = lax.broadcasted_iota(jnp.int32, (1, block), 1) + b % 2 * block
        live = ones_where(slot < count)
        sign = (1 - 2 * group).astype(jnp.float32)
        pick_own = ones_where(row_of == own_ids).astype(jnp.bfloat16)
        pick_other = ones_where(row_of == other_ids).astype(jnp.bfloat16)
        rel_row = lax.broadcasted_iota(jnp.int32, (relations.shape[1], block), 0)
        pick_rel = ones_where(rel_row == rel_ids).astype(jnp.bfloat16)

        def counts(ids):
            hits = ones_where(row_of == ids)
            hits = (hits[:, :LANES] + hits[:, LANES:]).astype(jnp.bfloat16)
            return product(hits, jnp.full((LANES, block), 1.0, jnp.bfloat16))

        mine = product(own[...], pick_own)
        theirs = product(other[...], pick_other)
        rel_re, rel_im = halves(product(relations[...], pick_rel))
        rel_im = rel_im * sign
        m_re, m_im = halves(mine)
        t_re, t_im = halves(theirs)
        u = jnp.concatenate([m_re * rel_re - m_im * rel_im, m_re * rel_im + m_im * rel_re], axis=0)
        v = jnp.concatenate([rel_re * t_re + rel_im * t_im, rel_re * t_im - rel_im * t_re], axis=0)
        u_low = u.astype(jnp.bfloat16)
        v_low = v.astype(jnp.bfloat16)
        positive = jnp.sum(u_low.astype(jnp.float32) * theirs, axis=0, keepdims=True)
        weight_pos = -jax.nn.sigmoid(-positive) * live
        share = live * (0.5 / rows)

        def weights(scores, ids):
            return ((1.0 + jnp.tanh(0.5 * scores)) * (counts(ids) * share)).astype(jnp.bfloat16)

        w_other = weights(product(other_rows[...], u_low), other_neg)
        w_own = weights(product(own_rows[...], v_low), own_neg)
        grad = weight_pos * theirs + product(other[...], w_other)
        g_re, g_im = halves(grad)
        grad = jnp.concatenate(
            [g_re * rel_re + g_im * rel_im, g_im * rel_re - g_re * rel_im], axis=0
        ).astype(jnp.bfloat16)
        total[...] += across_rows(grad, pick_own) + across_rows(v_low, w_own)
        return carry

    lax.fori_loop(0, 4, step, 0)
    for e in range(4):
        parts[e] = total[:, e * LANES : (e + 1) * LANES].astype(jnp.bfloat16)
    greeted(3)
    copies = [
        pltpu.make_async_remote_copy(
            parts.at[(edge + k) % 4],
            arrived.at[k - 1],
            send.at[k - 1],
            recv.at[k - 1],
            device_id=mates[k - 1],
            device_id_type=MESH,
        )
        for k in range(1, 4)
    ]
    for copy in copies:
        copy.start()
    for copy in copies:
        copy.wait()
    grad = parts[edge].astype(jnp.float32)
    for k in range(3):
        grad = grad + arrived[k].astype(jnp.float32)
    new_state = state[...] + jnp.sum(grad * grad, axis=0, keepdims=True) * (1.0 / width)
    new_table = table[...] - learning_rate * grad / jnp.sqrt(new_state)
    state_out[...] = new_state
    table_out[...] = new_table
    shard_out[...] = new_table.astype(jnp.bfloat16)


VMEM = pl.BlockSpec(memory_space=pltpu.VMEM)
DMA = pltpu.SemaphoreType.DMA
LIMIT = 24 * 2**20


def far(mask, shard, idx):
    width = shard.shape[0]
    return pl.pallas_call(
        functools.partial(far_kernel, mask),
        out_shape=(
            jax.ShapeDtypeStruct((width, 4 * LANES), jnp.bfloat16),
            jax.ShapeDtypeStruct(shard.shape, jnp.bfloat16),
            jax.ShapeDtypeStruct(idx.shape, jnp.int32),
        ),
        in_specs=[VMEM] * 2,
        out_specs=(VMEM,) * 3,
        scratch_shapes=[DMA((5,)), DMA((5,)), DMA((1,))],
        compiler_params=pltpu.CompilerParams(
            collective_id=mask, has_side_effects=True, vmem_limit_bytes=LIMIT
        ),
        name=f"far_{mask}",
    )(shard, idx)


def near(mask, shard, idx):
    width = shard.shape[0]
    return pl.pallas_call(
        functools.partial(near_kernel, mask),
        out_shape=(
            jax.ShapeDtypeStruct((width, 4 * LANES), jnp.bfloat16),
            jax.ShapeDtypeStruct(idx.shape, jnp.int32),
        ),
        in_specs=[VMEM] * 2,
        out_specs=(VMEM,) * 2,
        scratch_shapes=[DMA((5,)), DMA((5,)), DMA((1,))],
        compiler_params=pltpu.CompilerParams(
            collective_id=16 + mask, has_side_effects=True, vmem_limit_bytes=LIMIT
        ),
        name=f"near_{mask}",
    )(shard, idx)


def one_round(own, other, idx, other_idx, relations, table, state):
    width, rows = own.shape
    return pl.pallas_call(
        round_kernel,
        out_shape=(
            jax.ShapeDtypeStruct(table.shape, jnp.float32),
            jax.ShapeDtypeStruct(state.shape, jnp.float32),
            jax.ShapeDtypeStruct(table.shape, jnp.bfloat16),
        ),
        in_specs=[VMEM] * 7,
        out_specs=(VMEM,) * 3,
        scratch_shapes=[
            pltpu.VMEM((rows, width), jnp.bfloat16),
            pltpu.VMEM((rows, width), jnp.bfloat16),
            pltpu.VMEM((width, rows), jnp.float32),
            pltpu.VMEM((4, width, LANES), jnp.bfloat16),
            pltpu.VMEM((3, width, LANES), jnp.bfloat16),
            DMA((3,)),
            DMA((3,)),
        ],
        compiler_params=pltpu.CompilerParams(
            collective_id=24, has_side_effects=True, vmem_limit_bytes=LIMIT
        ),
        name="one_round",
    )(own, other, idx, other_idx, relations, table, state)


def packed_edges(own_ids, other_ids, rel_ids, own_neg, other_neg, count):
    rows = jnp.stack(
        [
            own_ids + other_ids * 65536,
            rel_ids + count * 65536,
            own_neg + other_neg * 65536,
        ]
    ).reshape(-1, LANES)
    return jnp.pad(rows, ((0, IDX_ROWS - rows.shape[0]), (0, 0)))


def on_device(
    embeddings, adagrad_state, relations, endpoints, relation_ids, negatives, edge_counts, plan
):
    table = embeddings.T
    shard = table.astype(jnp.bfloat16)
    state = adagrad_state[None, :]
    relations = relations.T
    for r in range(plan.shape[0]):
        ends = (endpoints[r, 0, 0], endpoints[r, 1, 0])
        negs = (negatives[r, 0, 0].reshape(-1), negatives[r, 1, 0].reshape(-1))
        rel_ids, count = relation_ids[r, 0], edge_counts[r, 0]
        here = packed_edges(ends[0], ends[1], rel_ids, negs[0], negs[1], count)
        away = packed_edges(ends[1], ends[0], rel_ids, negs[1], negs[0], count)
        high, low = plan[r] >> LOW_BITS, plan[r] & (2**LOW_BITS - 1)
        own, other, idx = lax.switch(
            high, [functools.partial(far, mask) for mask in range(16)], shard, away
        )
        other, idx = lax.switch(
            low, [functools.partial(near, mask) for mask in range(8)], other, idx
        )
        table, state, shard = one_round(own, other, here, idx, relations, table, state)
    return table.T, state[0]


def solution(mesh):
    in_specs = (
        P(("dom", "edge"), None),
        P(("dom", "edge")),
        P(),
        P(None, None, "dom", "edge"),
        P(None, "dom", "edge"),
        P(None, None, "dom", "edge", None),
        P(None, "dom", "edge"),
        P(),
    )
    out_specs = (P(("dom", "edge"), None), P(("dom", "edge")))
    return jax.shard_map(
        on_device, mesh=mesh, in_specs=in_specs, out_specs=out_specs, check_vma=False
    )
```

```python
import functools

import jax
import jax.numpy as jnp
from jax import lax
from jax.experimental import pallas as pl
from jax.experimental.pallas import tpu as pltpu
from jax.sharding import PartitionSpec as P

MESH = pl.DeviceIdType.MESH
learning_rate = 0.2
LANES = 128
LOW_BITS = 3
BLOCK = 256


def xor(value, mask):
    out = value
    for bit in range(mask.bit_length()):
        if mask >> bit & 1:
            out = out + (1 << bit) * (1 - 2 * (value // (1 << bit) % 2))
    return out


def columns(index):
    return pl.ds(pl.multiple_of(index * LANES, LANES), LANES)


def greet(devices):
    barrier = pltpu.get_barrier_semaphore()
    for device in devices:
        pl.semaphore_signal(barrier, inc=1, device_id=device, device_id_type=MESH)


def greeted(count):
    pl.semaphore_wait(pltpu.get_barrier_semaphore(), count)


def far_kernel(mask, mine, idx, own_full, other, other_idx, send, recv, local):
    dom, edge = lax.axis_index("dom"), lax.axis_index("edge")
    mates = [(dom, (edge + k) % 4) for k in range(1, 4)]
    across = (xor(dom, mask << LOW_BITS), edge)
    greet(mates + ([across] if mask else []))
    kept = pltpu.make_async_copy(mine, own_full.at[:, columns(edge)], local.at[0])
    kept.start()
    greeted(4 if mask else 3)
    copies = []
    if mask:
        for at, (src, dst) in enumerate(((mine, other), (idx, other_idx))):
            copies.append(
                pltpu.make_async_remote_copy(
                    src, dst, send.at[at], recv.at[at], device_id=across, device_id_type=MESH
                )
            )
    for k, mate in enumerate(mates):
        copies.append(
            pltpu.make_async_remote_copy(
                mine,
                own_full.at[:, columns(edge)],
                send.at[2 + k],
                recv.at[2 + k],
                device_id=mate,
                device_id_type=MESH,
            )
        )
    for copy in copies:
        copy.start()
    if not mask:
        other[...] = mine[...]
        other_idx[...] = idx[...]
    kept.wait()
    for copy in copies:
        copy.wait()


def pack_kernel(table, ends, rels, negs, counts, shard, *packed):
    shard[...] = table[...].astype(jnp.bfloat16)
    for r in range(2):
        here, away = packed[2 * r : 2 * r + 2]
        left, right = ends[r, 0], ends[r, 1]
        rel = rels[r] + counts[r] * 65536
        there, back = left + right * 65536, right + left * 65536
        for half in range(2):
            at = slice(half * BLOCK, (half + 1) * BLOCK)
            left_neg = negs[r, 0, 0, half : half + 1]
            right_neg = negs[r, 1, 0, half : half + 1]
            for out, ids, neg in (
                (here, there, left_neg + right_neg * 65536),
                (away, back, right_neg + left_neg * 65536),
            ):
                out[half : half + 1] = ids[:, at]
                out[2 + half : 3 + half] = rel[:, at]
                out[4 + half : 5 + half] = neg
        for out in (here, away):
            out[6:8] = jnp.zeros((2, BLOCK), jnp.int32)


def across_rows(left, right):
    return lax.dot_general(left, right, (((1,), (1,)), ((), ())), preferred_element_type=jnp.float32)


def product(left, right):
    return jnp.dot(left, right, preferred_element_type=jnp.float32)


def halves(values):
    half = values.shape[0] // 2
    return values[:half], values[half:]


def ones_where(condition):
    return jnp.where(condition, 1.0, 0.0)


CHUNKS = ((0, 208), (208, 192))


def near_kernel(mask, shard, idx, full, full_idx, send, recv, local):
    dom, edge = lax.axis_index("dom"), lax.axis_index("edge")
    chip, core = edge // 2, edge % 2
    partner = xor(dom, mask)
    other = (1 - chip) * 2 + core
    straight, crossed, sibling = (partner, edge), (partner, other), (dom, chip * 2 + (1 - core))
    greet([crossed, sibling] + ([straight] if mask else []))
    if not mask:
        kept = pltpu.make_async_copy(shard, full.at[:, columns(edge)], local.at[0])
        kept.start()
        full_idx[...] = idx[...]
    greeted(3 if mask else 2)

    def chunk(ref, piece, column):
        return ref.at[pl.ds(*CHUNKS[piece]), columns(column)]

    def moved(src, dst, at, device):
        return pltpu.make_async_remote_copy(
            src, dst, send.at[at], recv.at[at], device_id=device, device_id_type=MESH
        )

    away = [
        [
            moved(shard.at[pl.ds(*CHUNKS[piece]), :], chunk(full, piece, edge), 2 * piece + k, device)
            for k, device in enumerate((crossed, straight) if mask else (crossed,))
        ]
        for piece in range(2)
    ]
    ids = [moved(idx, full_idx, 8, straight)] if mask else []
    for copy in away[0] + ids + away[1]:
        copy.start()
    if not mask:
        kept.wait()
    forwards = []
    for piece in range(2):
        for k, copy in enumerate(away[piece]):
            copy.wait_recv()
            here = chunk(full, piece, edge if k else other)
            forwards.append(moved(here, here, 4 + 2 * piece + k, sibling))
            forwards[-1].start()
        if not mask:
            here = chunk(full, piece, edge)
            forwards.append(moved(here, here, 5 + 2 * piece, sibling))
            forwards[-1].start()
    for copy in away[0] + away[1]:
        copy.wait_send()
    for copy in ids + forwards:
        copy.wait()


def round_kernel(
    other, other_idx, own, here_idx, relations, table, state,
    table_out, state_out, shard_out,
    own_rows, other_rows, rel_kept, factors, grads, pick_own, weights_own, parts, arrived,
    send, recv,
):
    dom, edge = lax.axis_index("dom"), lax.axis_index("edge")
    chip, core = edge // 2, edge % 2
    sibling = (dom, chip * 2 + (1 - core))
    mates = [
        (dom, (1 - chip) * 2 + core),
        (dom, (1 - chip) * 2 + (1 - core)),
        sibling,
    ]
    greet(mates)
    width, rows = own.shape

    def ids_of(b, kind):
        ref = other_idx if b // 2 else here_idx
        return ref[2 * kind + b % 2 : 2 * kind + b % 2 + 1]

    def picked(ids, count):
        row_of = lax.broadcasted_iota(jnp.int32, (count, BLOCK), 0)
        return ones_where(row_of == ids).astype(jnp.bfloat16)

    def own_side(b):
        at = slice(b * BLOCK, (b + 1) * BLOCK)
        chosen = picked(ids_of(b, 0) & 65535, rows)
        pick_own[:, at] = chosen
        m_re, m_im = halves(product(own[...], chosen))
        pick_rel = picked(ids_of(b, 1) & 65535, relations.shape[1])
        rel_re, rel_im = halves(product(relations[...], pick_rel))
        if b // 2:
            rel_im = -rel_im
        rel_kept[:, at] = jnp.concatenate([rel_re, rel_im], axis=0).astype(jnp.bfloat16)
        grads[:, at] = jnp.concatenate(
            [m_re * rel_re - m_im * rel_im, m_re * rel_im + m_im * rel_re], axis=0
        ).astype(jnp.bfloat16)

    def weights(scores, ids, share):
        hits = picked(ids, rows)
        hits = product(hits[:, :LANES] + hits[:, LANES:], jnp.full((LANES, LANES), 1.0, jnp.bfloat16))
        hits = jnp.concatenate([hits, hits], axis=1) * share
        return ((1.0 + jnp.tanh(0.5 * scores)) * hits).astype(jnp.bfloat16)

    def both_sides(b):
        at = slice(b * BLOCK, (b + 1) * BLOCK)
        slot = lax.broadcasted_iota(jnp.int32, (1, BLOCK), 1) + b % 2 * BLOCK
        live = ones_where(slot < ids_of(b, 1) >> 16)
        share = live * (0.5 / rows)
        theirs = product(other[...], picked(ids_of(b, 0) >> 16, rows))
        rel_re, rel_im = halves(rel_kept[:, at].astype(jnp.float32))
        t_re, t_im = halves(theirs)
        u_low = grads[:, at]
        v_low = jnp.concatenate(
            [rel_re * t_re + rel_im * t_im, rel_re * t_im - rel_im * t_re], axis=0
        ).astype(jnp.bfloat16)
        factors[:, at] = v_low
        positive = jnp.sum(u_low.astype(jnp.float32) * theirs, axis=0, keepdims=True)
        weight_pos = -jax.nn.sigmoid(-positive) * live
        negs = ids_of(b, 2)
        w_other = weights(product(other_rows[...], u_low), negs >> 16, share)
        weights_own[:, at] = weights(product(own_rows[...], v_low), negs & 65535, share)
        grad = weight_pos * theirs + product(other[...], w_other)
        g_re, g_im = halves(grad)
        grads[:, at] = jnp.concatenate(
            [g_re * rel_re + g_im * rel_im, g_im * rel_re - g_re * rel_im], axis=0
        ).astype(jnp.bfloat16)

    own_rows[...] = own[...].T
    other_rows[...] = other[...].T
    for b in range(4):
        own_side(b)
        both_sides(b)

    def partial(which):
        at = pl.ds(pl.multiple_of(which * BLOCK, BLOCK), BLOCK)
        total = across_rows(grads[...], pick_own[at, :]) + across_rows(
            factors[...], weights_own[at, :]
        )
        total = total.astype(jnp.bfloat16)
        parts[2 * which] = total[:, :LANES]
        parts[2 * which + 1] = total[:, LANES:]

    gifts = [
        pltpu.make_async_remote_copy(
            parts.at[mate[1]],
            arrived.at[k],
            send.at[k],
            recv.at[k],
            device_id=mate,
            device_id_type=MESH,
        )
        for k, mate in enumerate(mates)
    ]
    partial(1 - chip)
    greeted(3)
    gifts[0].start()
    gifts[1].start()
    partial(chip)
    gifts[2].start()
    grad = parts[edge].astype(jnp.float32)
    for k in (2, 0, 1):
        gifts[k].wait_recv()
        grad = grad + arrived[k].astype(jnp.float32)
    new_state = state[...] + jnp.sum(grad * grad, axis=0, keepdims=True) * (1.0 / width)
    new_table = table[...] - learning_rate * grad / jnp.sqrt(new_state)
    shard_out[...] = new_table.astype(jnp.bfloat16)
    state_out[...] = new_state
    table_out[...] = new_table
    for copy in gifts:
        copy.wait_send()


VMEM = pl.BlockSpec(memory_space=pltpu.VMEM)
DMA = pltpu.SemaphoreType.DMA
LIMIT = 24 * 2**20


def shape(*dims, dtype=jnp.bfloat16):
    return jax.ShapeDtypeStruct(dims, dtype)


def like(array, dtype=None):
    return jax.ShapeDtypeStruct(array.shape, dtype or array.dtype)


def params(collective_id):
    return pltpu.CompilerParams(
        collective_id=collective_id, has_side_effects=True, vmem_limit_bytes=LIMIT
    )


def pack(table, ends, rels, negs, counts):
    idx = shape(8, BLOCK, dtype=jnp.int32)
    return pl.pallas_call(
        pack_kernel,
        out_shape=(like(table, jnp.bfloat16),) + (idx,) * 4,
        in_specs=[VMEM] * 5,
        out_specs=(VMEM,) * 5,
        compiler_params=pltpu.CompilerParams(vmem_limit_bytes=LIMIT),
        name="pack",
    )(table, ends, rels, negs, counts)


def far(mask, shard, idx):
    return pl.pallas_call(
        functools.partial(far_kernel, mask),
        out_shape=(shape(shard.shape[0], 4 * LANES), like(shard), like(idx)),
        in_specs=[VMEM] * 2,
        out_specs=(VMEM,) * 3,
        scratch_shapes=[DMA((5,)), DMA((5,)), DMA((1,))],
        compiler_params=params(mask),
        name=f"far_{mask}",
    )(shard, idx)


def near(mask, shard, idx):
    return pl.pallas_call(
        functools.partial(near_kernel, mask),
        out_shape=(shape(shard.shape[0], 4 * LANES), like(idx)),
        in_specs=[VMEM] * 2,
        out_specs=(VMEM,) * 2,
        scratch_shapes=[DMA((9,)), DMA((9,)), DMA((1,))],
        compiler_params=params(16 + mask),
        name=f"near_{mask}",
    )(shard, idx)


def one_round(other, other_idx, own, here_idx, relations, table, state):
    width, rows = own.shape
    low, edges = jnp.bfloat16, 4 * BLOCK
    return pl.pallas_call(
        round_kernel,
        out_shape=(like(table), like(state), like(table, low)),
        in_specs=[VMEM] * 7,
        out_specs=(VMEM,) * 3,
        scratch_shapes=[
            pltpu.VMEM((rows, width), low),
            pltpu.VMEM((rows, width), low),
            pltpu.VMEM((width, edges), low),
            pltpu.VMEM((width, edges), low),
            pltpu.VMEM((width, edges), low),
            pltpu.VMEM((rows, edges), low),
            pltpu.VMEM((rows, edges), low),
            pltpu.VMEM((4, width, LANES), low),
            pltpu.VMEM((3, width, LANES), low),
            DMA((3,)),
            DMA((3,)),
        ],
        compiler_params=params(24),
        name="one_round",
    )(other, other_idx, own, here_idx, relations, table, state)


def on_device(
    embeddings, adagrad_state, relations, endpoints, relation_ids, negatives, edge_counts, plan
):
    table = embeddings.T
    state = adagrad_state[None, :]
    relations = relations.T
    high, low = plan >> LOW_BITS, plan & (2**LOW_BITS - 1)
    shard, *packed = pack(table, endpoints, relation_ids, negatives, edge_counts)
    fars = [functools.partial(far, mask) for mask in range(16)]
    nears = [functools.partial(near, mask) for mask in range(8)]
    for r in range(plan.shape[0]):
        here, away = packed[2 * r : 2 * r + 2]
        own, other, idx = lax.switch(high[r], fars, shard, away)
        other, idx = lax.switch(low[r], nears, other, idx)
        table, state, shard = one_round(other, idx, own, here, relations, table, state)
    return table.T, state[0]


def solution(mesh):
    in_specs = (
        P(("dom", "edge"), None),
        P(("dom", "edge")),
        P(),
        P(None, None, "dom", "edge"),
        P(None, "dom", "edge"),
        P(None, None, "dom", "edge", None),
        P(None, "dom", "edge"),
        P(),
    )
    out_specs = (P(("dom", "edge"), None), P(("dom", "edge")))
    return jax.shard_map(
        on_device, mesh=mesh, in_specs=in_specs, out_specs=out_specs, check_vma=False
    )
```

```python
import functools

import jax
import jax.numpy as jnp
from jax import lax
from jax.experimental import pallas as pl
from jax.experimental.pallas import tpu as pltpu
from jax.sharding import PartitionSpec as P

MESH = pl.DeviceIdType.MESH
learning_rate = 0.2
LANES = 128
LOW_BITS = 3
BLOCK = 256


def xor(value, mask):
    out = value
    for bit in range(mask.bit_length()):
        if mask >> bit & 1:
            out = out + (1 << bit) * (1 - 2 * (value // (1 << bit) % 2))
    return out


def columns(index):
    return pl.ds(pl.multiple_of(index * LANES, LANES), LANES)


def greet(devices):
    barrier = pltpu.get_barrier_semaphore()
    for device in devices:
        pl.semaphore_signal(barrier, inc=1, device_id=device, device_id_type=MESH)


def greeted(count):
    pl.semaphore_wait(pltpu.get_barrier_semaphore(), count)


def far_kernel(mask, mine, idx, own_full, other, other_idx, send, recv, local):
    dom, edge = lax.axis_index("dom"), lax.axis_index("edge")
    mates = [(dom, (edge + k) % 4) for k in range(1, 4)]
    across = (xor(dom, mask << LOW_BITS), edge)
    greet(mates + ([across] if mask else []))
    kept = pltpu.make_async_copy(mine, own_full.at[:, columns(edge)], local.at[0])
    kept.start()
    greeted(4 if mask else 3)
    copies = []
    if mask:
        for at, (src, dst) in enumerate(((mine, other), (idx, other_idx))):
            copies.append(
                pltpu.make_async_remote_copy(
                    src, dst, send.at[at], recv.at[at], device_id=across, device_id_type=MESH
                )
            )
    for k, mate in enumerate(mates):
        copies.append(
            pltpu.make_async_remote_copy(
                mine,
                own_full.at[:, columns(edge)],
                send.at[2 + k],
                recv.at[2 + k],
                device_id=mate,
                device_id_type=MESH,
            )
        )
    for copy in copies:
        copy.start()
    if not mask:
        other[...] = mine[...]
        other_idx[...] = idx[...]
    kept.wait()
    for copy in copies:
        copy.wait()


def pack_kernel(*refs):
    given, (table_out, state_out, shard), packed = refs[:6], refs[6:9], refs[9:13]
    fetched, done = refs[13:17], refs[17]
    places = (table_out, state_out) + fetched
    copies = [
        pltpu.make_async_copy(src, dst, done.at[k])
        for k, (src, dst) in enumerate(zip(given, places))
    ]
    for copy in copies:
        copy.start()
    for copy in copies:
        copy.wait()
    ends, rels, negs, counts = fetched
    shard[...] = table_out[...].astype(jnp.bfloat16)
    for r in range(2):
        here, away = packed[2 * r : 2 * r + 2]
        left, right = ends[r, 0], ends[r, 1]
        rel = rels[r] + counts[:, r : r + 1] * 65536
        there, back = left + right * 65536, right + left * 65536
        for half in range(2):
            at = slice(half * BLOCK, (half + 1) * BLOCK)
            left_neg = negs[r, 0, 0, half : half + 1]
            right_neg = negs[r, 1, 0, half : half + 1]
            for out, ids, neg in (
                (here, there, left_neg + right_neg * 65536),
                (away, back, right_neg + left_neg * 65536),
            ):
                out[half : half + 1] = ids[:, at]
                out[2 + half : 3 + half] = rel[:, at]
                out[4 + half : 5 + half] = neg
        for out in (here, away):
            out[6:8] = jnp.zeros((2, BLOCK), jnp.int32)


def across_rows(left, right):
    return lax.dot_general(left, right, (((1,), (1,)), ((), ())), preferred_element_type=jnp.float32)


def product(left, right):
    return jnp.dot(left, right, preferred_element_type=jnp.float32)


def halves(values):
    half = values.shape[0] // 2
    return values[:half], values[half:]


def ones_where(condition):
    return jnp.where(condition, 1.0, 0.0)


CHUNKS = ((0, 208), (208, 192))


def near_kernel(mask, shard, idx, full, full_idx, send, recv, local):
    dom, edge = lax.axis_index("dom"), lax.axis_index("edge")
    chip, core = edge // 2, edge % 2
    partner = xor(dom, mask)
    other = (1 - chip) * 2 + core
    straight, crossed, sibling = (partner, edge), (partner, other), (dom, chip * 2 + (1 - core))
    greet([crossed, sibling] + ([straight] if mask else []))
    if not mask:
        kept = pltpu.make_async_copy(shard, full.at[:, columns(edge)], local.at[0])
        kept.start()
        full_idx[...] = idx[...]
    greeted(3 if mask else 2)

    def chunk(ref, piece, column):
        return ref.at[pl.ds(*CHUNKS[piece]), columns(column)]

    def moved(src, dst, at, device):
        return pltpu.make_async_remote_copy(
            src, dst, send.at[at], recv.at[at], device_id=device, device_id_type=MESH
        )

    away = [
        [
            moved(shard.at[pl.ds(*CHUNKS[piece]), :], chunk(full, piece, edge), 2 * piece + k, device)
            for k, device in enumerate((crossed, straight) if mask else (crossed,))
        ]
        for piece in range(2)
    ]
    ids = [moved(idx, full_idx, 8, straight)] if mask else []
    for copy in away[0] + ids + away[1]:
        copy.start()
    if not mask:
        kept.wait()
    forwards = []
    for piece in range(2):
        for k, copy in enumerate(away[piece]):
            copy.wait_recv()
            here = chunk(full, piece, edge if k else other)
            forwards.append(moved(here, here, 4 + 2 * piece + k, sibling))
            forwards[-1].start()
        if not mask:
            here = chunk(full, piece, edge)
            forwards.append(moved(here, here, 5 + 2 * piece, sibling))
            forwards[-1].start()
    for copy in away[0] + away[1]:
        copy.wait_send()
    for copy in ids + forwards:
        copy.wait()


def round_kernel(
    other, other_idx, own, here_idx, relations, table, state,
    table_out, state_out, shard_out,
    own_rows, other_rows, rel_kept, factors, grads, pick_own, weights_own, totals, parts, chip_sum, arrived,
    send, recv,
):
    dom, edge = lax.axis_index("dom"), lax.axis_index("edge")
    chip, core = edge // 2, edge % 2
    sibling = (dom, chip * 2 + (1 - core))
    across = (dom, (1 - chip) * 2 + core)
    greet([across, sibling])
    width, rows = own.shape

    def ids_of(b, kind):
        ref = other_idx if b // 2 else here_idx
        return ref[2 * kind + b % 2 : 2 * kind + b % 2 + 1]

    def picked(ids, count):
        row_of = lax.broadcasted_iota(jnp.int32, (count, BLOCK), 0)
        return ones_where(row_of == ids).astype(jnp.bfloat16)

    def own_side(b):
        at = slice(b * BLOCK, (b + 1) * BLOCK)
        chosen = picked(ids_of(b, 0) & 65535, rows)
        pick_own[:, at] = chosen
        m_re, m_im = halves(product(own[...], chosen))
        pick_rel = picked(ids_of(b, 1) & 65535, relations.shape[1])
        rel_re, rel_im = halves(product(relations[...], pick_rel))
        if b // 2:
            rel_im = -rel_im
        rel_kept[:, at] = jnp.concatenate([rel_re, rel_im], axis=0).astype(jnp.bfloat16)
        grads[:, at] = jnp.concatenate(
            [m_re * rel_re - m_im * rel_im, m_re * rel_im + m_im * rel_re], axis=0
        ).astype(jnp.bfloat16)

    def weights(scores, ids, share):
        hits = picked(ids, rows)
        hits = product(hits[:, :LANES] + hits[:, LANES:], jnp.full((LANES, LANES), 1.0, jnp.bfloat16))
        hits = jnp.concatenate([hits, hits], axis=1) * share
        return ((1.0 + jnp.tanh(0.5 * scores)) * hits).astype(jnp.bfloat16)

    def both_sides(b):
        at = slice(b * BLOCK, (b + 1) * BLOCK)
        slot = lax.broadcasted_iota(jnp.int32, (1, BLOCK), 1) + b % 2 * BLOCK
        live = ones_where(slot < ids_of(b, 1) >> 16)
        share = live * (0.5 / rows)
        theirs = product(other[...], picked(ids_of(b, 0) >> 16, rows))
        rel_re, rel_im = halves(rel_kept[:, at].astype(jnp.float32))
        t_re, t_im = halves(theirs)
        u_low = grads[:, at]
        v_low = jnp.concatenate(
            [rel_re * t_re + rel_im * t_im, rel_re * t_im - rel_im * t_re], axis=0
        ).astype(jnp.bfloat16)
        factors[:, at] = v_low
        positive = jnp.sum(u_low.astype(jnp.float32) * theirs, axis=0, keepdims=True)
        weight_pos = -jax.nn.sigmoid(-positive) * live
        negs = ids_of(b, 2)
        w_other = weights(product(other_rows[...], u_low), negs >> 16, share)
        weights_own[:, at] = weights(product(own_rows[...], v_low), negs & 65535, share)
        grad = weight_pos * theirs + product(other[...], w_other)
        g_re, g_im = halves(grad)
        grads[:, at] = jnp.concatenate(
            [g_re * rel_re + g_im * rel_im, g_im * rel_re - g_re * rel_im], axis=0
        ).astype(jnp.bfloat16)

    own_rows[...] = own[...].T
    other_rows[...] = other[...].T
    for b in range(4):
        own_side(b)
        both_sides(b)

    def partial(which, kept):
        at = pl.ds(pl.multiple_of(which * BLOCK, BLOCK), BLOCK)
        total = across_rows(grads[...], pick_own[at, :]) + across_rows(
            factors[...], weights_own[at, :]
        )
        for c in range(2):
            half = total[:, c * LANES : (c + 1) * LANES]
            totals[kept, c] = half
            parts[kept, c] = half.astype(jnp.bfloat16)

    def given(src, at, device):
        return pltpu.make_async_remote_copy(
            src, arrived.at[at], send.at[at], recv.at[at], device_id=device, device_id_type=MESH
        )

    gifts = [
        given(parts.at[0, 1 - core], 0, sibling),
        given(parts.at[1, 1 - core], 1, sibling),
        given(chip_sum, 2, across),
    ]
    partial(1 - chip, 0)
    greeted(2)
    gifts[0].start()
    partial(chip, 1)
    gifts[1].start()
    gifts[0].wait_recv()
    chip_sum[...] = (totals[0, core] + arrived[0].astype(jnp.float32)).astype(jnp.bfloat16)
    gifts[2].start()
    gifts[1].wait_recv()
    grad = totals[1, core] + arrived[1].astype(jnp.float32)
    gifts[2].wait_recv()
    grad = grad + arrived[2].astype(jnp.float32)
    new_state = state[...] + jnp.sum(grad * grad, axis=0, keepdims=True) * (1.0 / width)
    new_table = table[...] - learning_rate * grad / jnp.sqrt(new_state)
    shard_out[...] = new_table.astype(jnp.bfloat16)
    state_out[...] = new_state
    table_out[...] = new_table
    for copy in gifts:
        copy.wait_send()


VMEM = pl.BlockSpec(memory_space=pltpu.VMEM)
DMA = pltpu.SemaphoreType.DMA
LIMIT = 24 * 2**20


def shape(*dims, dtype=jnp.bfloat16):
    return jax.ShapeDtypeStruct(dims, dtype)


def like(array, dtype=None):
    return jax.ShapeDtypeStruct(array.shape, dtype or array.dtype)


def params(collective_id):
    return pltpu.CompilerParams(
        collective_id=collective_id, has_side_effects=True, vmem_limit_bytes=LIMIT
    )


def pack(table, state, ends, rels, negs, counts):
    idx = shape(8, BLOCK, dtype=jnp.int32)
    rest = (ends, rels, negs, counts)
    return pl.pallas_call(
        pack_kernel,
        out_shape=(like(table), like(state), like(table, jnp.bfloat16)) + (idx,) * 4,
        in_specs=[pl.BlockSpec(memory_space=pl.ANY)] * 6,
        out_specs=(VMEM,) * 7,
        scratch_shapes=[pltpu.VMEM(a.shape, a.dtype) for a in rest] + [DMA((6,))],
        compiler_params=pltpu.CompilerParams(vmem_limit_bytes=LIMIT),
        name="pack",
    )(table, state, *rest)


def hand_over_kernel(table, state, table_out, state_out):
    table_out[...] = table[...]
    state_out[...] = state[...]


def hand_over(table, state):
    return pl.pallas_call(
        hand_over_kernel,
        out_shape=(like(table), like(state)),
        in_specs=[VMEM] * 2,
        out_specs=(VMEM,) * 2,
        compiler_params=pltpu.CompilerParams(vmem_limit_bytes=LIMIT),
        name="hand_over",
    )(table, state)


def far(mask, shard, idx):
    return pl.pallas_call(
        functools.partial(far_kernel, mask),
        out_shape=(shape(shard.shape[0], 4 * LANES), like(shard), like(idx)),
        in_specs=[VMEM] * 2,
        out_specs=(VMEM,) * 3,
        scratch_shapes=[DMA((5,)), DMA((5,)), DMA((1,))],
        compiler_params=params(mask),
        name=f"far_{mask}",
    )(shard, idx)


def near(mask, shard, idx):
    return pl.pallas_call(
        functools.partial(near_kernel, mask),
        out_shape=(shape(shard.shape[0], 4 * LANES), like(idx)),
        in_specs=[VMEM] * 2,
        out_specs=(VMEM,) * 2,
        scratch_shapes=[DMA((9,)), DMA((9,)), DMA((1,))],
        compiler_params=params(16 + mask),
        name=f"near_{mask}",
    )(shard, idx)


def one_round(other, other_idx, own, here_idx, relations, table, state):
    width, rows = own.shape
    low, edges = jnp.bfloat16, 4 * BLOCK
    return pl.pallas_call(
        round_kernel,
        out_shape=(like(table), like(state), like(table, low)),
        in_specs=[VMEM] * 7,
        out_specs=(VMEM,) * 3,
        scratch_shapes=[
            pltpu.VMEM((rows, width), low),
            pltpu.VMEM((rows, width), low),
            pltpu.VMEM((width, edges), low),
            pltpu.VMEM((width, edges), low),
            pltpu.VMEM((width, edges), low),
            pltpu.VMEM((rows, edges), low),
            pltpu.VMEM((rows, edges), low),
            pltpu.VMEM((2, 2, width, LANES), jnp.float32),
            pltpu.VMEM((2, 2, width, LANES), low),
            pltpu.VMEM((width, LANES), low),
            pltpu.VMEM((3, width, LANES), low),
            DMA((3,)),
            DMA((3,)),
        ],
        compiler_params=params(24),
        name="one_round",
    )(other, other_idx, own, here_idx, relations, table, state)


def on_device(
    embeddings, adagrad_state, relations, endpoints, relation_ids, negatives, edge_counts, plan
):
    table = embeddings.T
    state = adagrad_state[None, :]
    relations = relations.T
    high, low = plan >> LOW_BITS, plan & (2**LOW_BITS - 1)
    table, state, shard, *packed = pack(
        table, state, endpoints, relation_ids, negatives, edge_counts.reshape(1, -1)
    )
    fars = [functools.partial(far, mask) for mask in range(16)]
    nears = [functools.partial(near, mask) for mask in range(8)]
    for r in range(plan.shape[0]):
        here, away = packed[2 * r : 2 * r + 2]
        own, other, idx = lax.switch(high[r], fars, shard, away)
        other, idx = lax.switch(low[r], nears, other, idx)
        table, state, shard = one_round(other, idx, own, here, relations, table, state)
    table, state = hand_over(table, state)
    return table.T, state[0]


def solution(mesh):
    in_specs = (
        P(("dom", "edge"), None),
        P(("dom", "edge")),
        P(),
        P(None, None, "dom", "edge"),
        P(None, "dom", "edge"),
        P(None, None, "dom", "edge", None),
        P(None, "dom", "edge"),
        P(),
    )
    out_specs = (P(("dom", "edge"), None), P(("dom", "edge")))
    return jax.shard_map(
        on_device, mesh=mesh, in_specs=in_specs, out_specs=out_specs, check_vma=False
    )
```

```python
import functools

import jax
import jax.numpy as jnp
from jax import lax
from jax.experimental import pallas as pl
from jax.experimental.pallas import tpu as pltpu
from jax.sharding import PartitionSpec as P

MESH = pl.DeviceIdType.MESH
learning_rate = 0.2
LANES = 128
LOW_BITS = 3
BLOCK = 256


CHUNKS = ((0, 208), (208, 192))


def xor(value, mask):
    out = value
    for bit in range(mask.bit_length()):
        if mask >> bit & 1:
            out = out + (1 << bit) * (1 - 2 * (value // (1 << bit) % 2))
    return out


def columns(index):
    return pl.ds(pl.multiple_of(index * LANES, LANES), LANES)


def greet(devices):
    barrier = pltpu.get_barrier_semaphore()
    for device in devices:
        pl.semaphore_signal(barrier, inc=1, device_id=device, device_id_type=MESH)


def greeted(count):
    pl.semaphore_wait(pltpu.get_barrier_semaphore(), count)


def far_kernel(mask, mine, idx, own_full, other, other_idx, send, recv, local):
    dom, edge = lax.axis_index("dom"), lax.axis_index("edge")
    mates = [(dom, (edge + k) % 4) for k in range(1, 4)]
    across = (xor(dom, mask << LOW_BITS), edge)
    greet(([across] if mask else []) + mates)
    kept = pltpu.make_async_copy(mine, own_full.at[:, columns(edge)], local.at[0])
    kept.start()
    greeted(4 if mask else 3)
    copies = []
    if mask:
        pieces = [(mine.at[pl.ds(*c), :], other.at[pl.ds(*c), :]) for c in CHUNKS]
        for at, (src, dst) in enumerate(pieces + [(idx, other_idx)]):
            copies.append(
                pltpu.make_async_remote_copy(
                    src, dst, send.at[at], recv.at[at], device_id=across, device_id_type=MESH
                )
            )
    for k, mate in enumerate(mates):
        copies.append(
            pltpu.make_async_remote_copy(
                mine,
                own_full.at[:, columns(edge)],
                send.at[3 + k],
                recv.at[3 + k],
                device_id=mate,
                device_id_type=MESH,
            )
        )
    for copy in copies:
        copy.start()
    if not mask:
        other[...] = mine[...]
        other_idx[...] = idx[...]
    kept.wait()
    for copy in copies:
        copy.wait()


def pack_kernel(*refs):
    given, (table_out, state_out, shard), packed = refs[:6], refs[6:9], refs[9:13]
    fetched, done = refs[13:17], refs[17]
    places = (table_out, state_out) + fetched
    copies = [
        pltpu.make_async_copy(src, dst, done.at[k])
        for k, (src, dst) in enumerate(zip(given, places))
    ]
    for copy in copies:
        copy.start()
    for copy in copies:
        copy.wait()
    ends, rels, negs, counts = fetched
    shard[...] = table_out[...].astype(jnp.bfloat16)
    for r in range(2):
        here, away = packed[2 * r : 2 * r + 2]
        left, right = ends[r, 0], ends[r, 1]
        rel = rels[r] + counts[:, r : r + 1] * 65536
        there, back = left + right * 65536, right + left * 65536
        for half in range(2):
            at = slice(half * BLOCK, (half + 1) * BLOCK)
            left_neg = negs[r, 0, 0, half : half + 1]
            right_neg = negs[r, 1, 0, half : half + 1]
            for out, ids, neg in (
                (here, there, left_neg + right_neg * 65536),
                (away, back, right_neg + left_neg * 65536),
            ):
                out[half : half + 1] = ids[:, at]
                out[2 + half : 3 + half] = rel[:, at]
                out[4 + half : 5 + half] = neg
        for out in (here, away):
            out[6:8] = jnp.zeros((2, BLOCK), jnp.int32)


def across_rows(left, right):
    return lax.dot_general(left, right, (((1,), (1,)), ((), ())), preferred_element_type=jnp.float32)


def product(left, right):
    return jnp.dot(left, right, preferred_element_type=jnp.float32)


def halves(values):
    half = values.shape[0] // 2
    return values[:half], values[half:]


def ones_where(condition):
    return jnp.where(condition, 1.0, 0.0)


def near_kernel(mask, shard, idx, full, full_idx, send, recv, local):
    dom, edge = lax.axis_index("dom"), lax.axis_index("edge")
    chip, core = edge // 2, edge % 2
    partner = xor(dom, mask)
    other = (1 - chip) * 2 + core
    straight, crossed, sibling = (partner, edge), (partner, other), (dom, chip * 2 + (1 - core))
    greet(([straight] if mask else []) + [crossed, sibling])
    if not mask:
        kept = pltpu.make_async_copy(shard, full.at[:, columns(edge)], local.at[0])
        kept.start()
        full_idx[...] = idx[...]
    greeted(3 if mask else 2)

    def chunk(ref, piece, column):
        return ref.at[pl.ds(*CHUNKS[piece]), columns(column)]

    def moved(src, dst, at, device):
        return pltpu.make_async_remote_copy(
            src, dst, send.at[at], recv.at[at], device_id=device, device_id_type=MESH
        )

    away = [
        [
            moved(shard.at[pl.ds(*CHUNKS[piece]), :], chunk(full, piece, edge), 2 * piece + k, device)
            for k, device in enumerate((crossed, straight) if mask else (crossed,))
        ]
        for piece in range(2)
    ]
    ids = [moved(idx, full_idx, 8, straight)] if mask else []
    for copy in away[0] + ids + away[1]:
        copy.start()
    if not mask:
        kept.wait()
    forwards = []
    for piece in range(2):
        for k, copy in enumerate(away[piece]):
            copy.wait_recv()
            here = chunk(full, piece, edge if k else other)
            forwards.append(moved(here, here, 4 + 2 * piece + k, sibling))
            forwards[-1].start()
        if not mask:
            here = chunk(full, piece, edge)
            forwards.append(moved(here, here, 5 + 2 * piece, sibling))
            forwards[-1].start()
    for copy in away[0] + away[1]:
        copy.wait_send()
    for copy in ids + forwards:
        copy.wait()


def round_kernel(
    other, other_idx, own, here_idx, relations, table, state,
    table_out, state_out, shard_out,
    own_rows, other_rows, rel_kept, factors, grads, pick_own, weights_own, totals, parts, chip_sum, arrived,
    send, recv,
):
    dom, edge = lax.axis_index("dom"), lax.axis_index("edge")
    chip, core = edge // 2, edge % 2
    sibling = (dom, chip * 2 + (1 - core))
    across = (dom, (1 - chip) * 2 + core)
    greet([across, sibling])
    width, rows = own.shape

    def ids_of(b, kind):
        ref = other_idx if b // 2 else here_idx
        return ref[2 * kind + b % 2 : 2 * kind + b % 2 + 1]

    def picked(ids, count):
        row_of = lax.broadcasted_iota(jnp.int32, (count, BLOCK), 0)
        return ones_where(row_of == ids).astype(jnp.bfloat16)

    def own_side(b):
        at = slice(b * BLOCK, (b + 1) * BLOCK)
        chosen = picked(ids_of(b, 0) & 65535, rows)
        pick_own[:, at] = chosen
        m_re, m_im = halves(product(own[...], chosen))
        pick_rel = picked(ids_of(b, 1) & 65535, relations.shape[1])
        rel_re, rel_im = halves(product(relations[...], pick_rel))
        if b // 2:
            rel_im = -rel_im
        rel_kept[:, at] = jnp.concatenate([rel_re, rel_im], axis=0).astype(jnp.bfloat16)
        grads[:, at] = jnp.concatenate(
            [m_re * rel_re - m_im * rel_im, m_re * rel_im + m_im * rel_re], axis=0
        ).astype(jnp.bfloat16)

    def weights(scores, ids, share):
        hits = picked(ids, rows)
        hits = product(hits[:, :LANES] + hits[:, LANES:], jnp.full((LANES, LANES), 1.0, jnp.bfloat16))
        hits = jnp.concatenate([hits, hits], axis=1) * share
        return ((1.0 + jnp.tanh(0.5 * scores)) * hits).astype(jnp.bfloat16)

    def both_sides(b):
        at = slice(b * BLOCK, (b + 1) * BLOCK)
        slot = lax.broadcasted_iota(jnp.int32, (1, BLOCK), 1) + b % 2 * BLOCK
        live = ones_where(slot < ids_of(b, 1) >> 16)
        share = live * (0.5 / rows)
        theirs = product(other[...], picked(ids_of(b, 0) >> 16, rows))
        rel_re, rel_im = halves(rel_kept[:, at].astype(jnp.float32))
        t_re, t_im = halves(theirs)
        u_low = grads[:, at]
        v_low = jnp.concatenate(
            [rel_re * t_re + rel_im * t_im, rel_re * t_im - rel_im * t_re], axis=0
        ).astype(jnp.bfloat16)
        factors[:, at] = v_low
        positive = jnp.sum(u_low.astype(jnp.float32) * theirs, axis=0, keepdims=True)
        weight_pos = -jax.nn.sigmoid(-positive) * live
        negs = ids_of(b, 2)
        w_other = weights(product(other_rows[...], u_low), negs >> 16, share)
        weights_own[:, at] = weights(product(own_rows[...], v_low), negs & 65535, share)
        grad = weight_pos * theirs + product(other[...], w_other)
        g_re, g_im = halves(grad)
        grads[:, at] = jnp.concatenate(
            [g_re * rel_re + g_im * rel_im, g_im * rel_re - g_re * rel_im], axis=0
        ).astype(jnp.bfloat16)

    own_rows[...] = own[...].T
    other_rows[...] = other[...].T
    for b in range(4):
        own_side(b)
        both_sides(b)

    def partial(which, kept):
        at = pl.ds(pl.multiple_of(which * BLOCK, BLOCK), BLOCK)
        total = across_rows(grads[...], pick_own[at, :]) + across_rows(
            factors[...], weights_own[at, :]
        )
        for c in range(2):
            half = total[:, c * LANES : (c + 1) * LANES]
            totals[kept, c] = half
            parts[kept, c] = half.astype(jnp.bfloat16)

    def given(src, at, device):
        return pltpu.make_async_remote_copy(
            src, arrived.at[at], send.at[at], recv.at[at], device_id=device, device_id_type=MESH
        )

    gifts = [
        given(parts.at[0, 1 - core], 0, sibling),
        given(parts.at[1, 1 - core], 1, sibling),
        given(chip_sum, 2, across),
    ]
    partial(1 - chip, 0)
    greeted(2)
    gifts[0].start()
    partial(chip, 1)
    gifts[1].start()
    gifts[0].wait_recv()
    chip_sum[...] = (totals[0, core] + arrived[0].astype(jnp.float32)).astype(jnp.bfloat16)
    gifts[2].start()
    gifts[1].wait_recv()
    grad = totals[1, core] + arrived[1].astype(jnp.float32)
    gifts[2].wait_recv()
    grad = grad + arrived[2].astype(jnp.float32)
    new_state = state[...] + jnp.sum(grad * grad, axis=0, keepdims=True) * (1.0 / width)
    new_table = table[...] - learning_rate * grad / jnp.sqrt(new_state)
    shard_out[...] = new_table.astype(jnp.bfloat16)
    state_out[...] = new_state
    table_out[...] = new_table
    for copy in gifts:
        copy.wait_send()


VMEM = pl.BlockSpec(memory_space=pltpu.VMEM)
DMA = pltpu.SemaphoreType.DMA
LIMIT = 24 * 2**20


def shape(*dims, dtype=jnp.bfloat16):
    return jax.ShapeDtypeStruct(dims, dtype)


def like(array, dtype=None):
    return jax.ShapeDtypeStruct(array.shape, dtype or array.dtype)


def params(collective_id):
    return pltpu.CompilerParams(
        collective_id=collective_id, has_side_effects=True, vmem_limit_bytes=LIMIT
    )


def pack(table, state, ends, rels, negs, counts):
    idx = shape(8, BLOCK, dtype=jnp.int32)
    rest = (ends, rels, negs, counts)
    return pl.pallas_call(
        pack_kernel,
        out_shape=(like(table), like(state), like(table, jnp.bfloat16)) + (idx,) * 4,
        in_specs=[pl.BlockSpec(memory_space=pl.ANY)] * 6,
        out_specs=(VMEM,) * 7,
        scratch_shapes=[pltpu.VMEM(a.shape, a.dtype) for a in rest] + [DMA((6,))],
        compiler_params=pltpu.CompilerParams(vmem_limit_bytes=LIMIT),
        name="pack",
    )(table, state, *rest)


def hand_over_kernel(table, state, table_out, state_out):
    table_out[...] = table[...]
    state_out[...] = state[...]


def hand_over(table, state):
    return pl.pallas_call(
        hand_over_kernel,
        out_shape=(like(table), like(state)),
        in_specs=[VMEM] * 2,
        out_specs=(VMEM,) * 2,
        compiler_params=pltpu.CompilerParams(vmem_limit_bytes=LIMIT),
        name="hand_over",
    )(table, state)


def far(mask, shard, idx):
    return pl.pallas_call(
        functools.partial(far_kernel, mask),
        out_shape=(shape(shard.shape[0], 4 * LANES), like(shard), like(idx)),
        in_specs=[VMEM] * 2,
        out_specs=(VMEM,) * 3,
        scratch_shapes=[DMA((6,)), DMA((6,)), DMA((1,))],
        compiler_params=params(mask),
        name=f"far_{mask}",
    )(shard, idx)


def near(mask, shard, idx):
    return pl.pallas_call(
        functools.partial(near_kernel, mask),
        out_shape=(shape(shard.shape[0], 4 * LANES), like(idx)),
        in_specs=[VMEM] * 2,
        out_specs=(VMEM,) * 2,
        scratch_shapes=[DMA((9,)), DMA((9,)), DMA((1,))],
        compiler_params=params(16 + mask),
        name=f"near_{mask}",
    )(shard, idx)


def one_round(other, other_idx, own, here_idx, relations, table, state):
    width, rows = own.shape
    low, edges = jnp.bfloat16, 4 * BLOCK
    return pl.pallas_call(
        round_kernel,
        out_shape=(like(table), like(state), like(table, low)),
        in_specs=[VMEM] * 7,
        out_specs=(VMEM,) * 3,
        scratch_shapes=[
            pltpu.VMEM((rows, width), low),
            pltpu.VMEM((rows, width), low),
            pltpu.VMEM((width, edges), low),
            pltpu.VMEM((width, edges), low),
            pltpu.VMEM((width, edges), low),
            pltpu.VMEM((rows, edges), low),
            pltpu.VMEM((rows, edges), low),
            pltpu.VMEM((2, 2, width, LANES), jnp.float32),
            pltpu.VMEM((2, 2, width, LANES), low),
            pltpu.VMEM((width, LANES), low),
            pltpu.VMEM((3, width, LANES), low),
            DMA((3,)),
            DMA((3,)),
        ],
        compiler_params=params(24),
        name="one_round",
    )(other, other_idx, own, here_idx, relations, table, state)


def on_device(
    embeddings, adagrad_state, relations, endpoints, relation_ids, negatives, edge_counts, plan
):
    table = embeddings.T
    state = adagrad_state[None, :]
    relations = relations.T
    high, low = plan >> LOW_BITS, plan & (2**LOW_BITS - 1)
    table, state, shard, *packed = pack(
        table, state, endpoints, relation_ids, negatives, edge_counts.reshape(1, -1)
    )
    fars = [functools.partial(far, mask) for mask in range(16)]
    nears = [functools.partial(near, mask) for mask in range(8)]
    for r in range(plan.shape[0]):
        here, away = packed[2 * r : 2 * r + 2]
        own, other, idx = lax.switch(high[r], fars, shard, away)
        other, idx = lax.switch(low[r], nears, other, idx)
        table, state, shard = one_round(other, idx, own, here, relations, table, state)
    table, state = hand_over(table, state)
    return table.T, state[0]


def solution(mesh):
    in_specs = (
        P(("dom", "edge"), None),
        P(("dom", "edge")),
        P(),
        P(None, None, "dom", "edge"),
        P(None, "dom", "edge"),
        P(None, None, "dom", "edge", None),
        P(None, "dom", "edge"),
        P(),
    )
    out_specs = (P(("dom", "edge"), None), P(("dom", "edge")))
    return jax.shard_map(
        on_device, mesh=mesh, in_specs=in_specs, out_specs=out_specs, check_vma=False
    )
```

```python
import functools

import jax
import jax.numpy as jnp
from jax import lax
from jax.experimental import pallas as pl
from jax.experimental.pallas import tpu as pltpu
from jax.sharding import PartitionSpec as P

MESH = pl.DeviceIdType.MESH
learning_rate = 0.2
LANES = 128
LOW_BITS = 3
BLOCK = 256


CHUNKS = ((0, 208), (208, 192))


def xor(value, mask):
    out = value
    for bit in range(mask.bit_length()):
        if mask >> bit & 1:
            out = out + (1 << bit) * (1 - 2 * (value // (1 << bit) % 2))
    return out


def columns(index):
    return pl.ds(pl.multiple_of(index * LANES, LANES), LANES)


def greet(devices):
    barrier = pltpu.get_barrier_semaphore()
    for device in devices:
        pl.semaphore_signal(barrier, inc=1, device_id=device, device_id_type=MESH)


def greeted(count):
    pl.semaphore_wait(pltpu.get_barrier_semaphore(), count)


def far_kernel(mask, mine, idx, own_full, other, other_idx, send, recv, local):
    dom, edge = lax.axis_index("dom"), lax.axis_index("edge")
    mates = [(dom, (edge + k) % 4) for k in range(1, 4)]
    across = (xor(dom, mask << LOW_BITS), edge)
    greet(([across] if mask else []) + mates)
    kept = pltpu.make_async_copy(mine, own_full.at[:, columns(edge)], local.at[0])
    kept.start()
    greeted(4 if mask else 3)
    copies = []
    if mask:
        pieces = [(mine.at[pl.ds(*c), :], other.at[pl.ds(*c), :]) for c in CHUNKS]
        for at, (src, dst) in enumerate(pieces + [(idx, other_idx)]):
            copies.append(
                pltpu.make_async_remote_copy(
                    src, dst, send.at[at], recv.at[at], device_id=across, device_id_type=MESH
                )
            )
    for k, mate in enumerate(mates):
        copies.append(
            pltpu.make_async_remote_copy(
                mine,
                own_full.at[:, columns(edge)],
                send.at[3 + k],
                recv.at[3 + k],
                device_id=mate,
                device_id_type=MESH,
            )
        )
    for copy in copies:
        copy.start()
    if not mask:
        other[...] = mine[...]
        other_idx[...] = idx[...]
    kept.wait()
    for copy in copies:
        copy.wait()


def pack_kernel(*refs):
    given, (table_out, state_out, shard), packed = refs[:6], refs[6:9], refs[9:13]
    fetched, done = refs[13:17], refs[17]
    places = (table_out, state_out) + fetched
    copies = [
        pltpu.make_async_copy(src, dst, done.at[k])
        for k, (src, dst) in enumerate(zip(given, places))
    ]
    for copy in copies:
        copy.start()
    for copy in copies:
        copy.wait()
    ends, rels, negs, counts = fetched
    shard[...] = table_out[...].astype(jnp.bfloat16)
    for r in range(2):
        here, away = packed[2 * r : 2 * r + 2]
        left, right = ends[r, 0], ends[r, 1]
        rel = rels[r] + counts[:, r : r + 1] * 65536
        there, back = left + right * 65536, right + left * 65536
        for half in range(2):
            at = slice(half * BLOCK, (half + 1) * BLOCK)
            left_neg = negs[r, 0, 0, half : half + 1]
            right_neg = negs[r, 1, 0, half : half + 1]
            for out, ids, neg in (
                (here, there, left_neg + right_neg * 65536),
                (away, back, right_neg + left_neg * 65536),
            ):
                out[half : half + 1] = ids[:, at]
                out[2 + half : 3 + half] = rel[:, at]
                out[4 + half : 5 + half] = neg
        for out in (here, away):
            out[6:8] = jnp.zeros((2, BLOCK), jnp.int32)


def across_rows(left, right):
    return lax.dot_general(left, right, (((1,), (1,)), ((), ())), preferred_element_type=jnp.float32)


def product(left, right):
    return jnp.dot(left, right, preferred_element_type=jnp.float32)


def halves(values):
    half = values.shape[0] // 2
    return values[:half], values[half:]


def ones_where(condition):
    return jnp.where(condition, 1.0, 0.0)


def near_kernel(mask, shard, idx, full, full_idx, send, recv, local):
    dom, edge = lax.axis_index("dom"), lax.axis_index("edge")
    chip, core = edge // 2, edge % 2
    partner = xor(dom, mask)
    other = (1 - chip) * 2 + core
    straight, crossed, sibling = (partner, edge), (partner, other), (dom, chip * 2 + (1 - core))
    greet(([straight] if mask else []) + [crossed, sibling])
    if not mask:
        kept = pltpu.make_async_copy(shard, full.at[:, columns(edge)], local.at[0])
        kept.start()
        full_idx[...] = idx[...]
    greeted(3 if mask else 2)

    def chunk(ref, piece, column):
        return ref.at[pl.ds(*CHUNKS[piece]), columns(column)]

    def moved(src, dst, at, device):
        return pltpu.make_async_remote_copy(
            src, dst, send.at[at], recv.at[at], device_id=device, device_id_type=MESH
        )

    away = [
        [
            moved(shard.at[pl.ds(*CHUNKS[piece]), :], chunk(full, piece, edge), 2 * piece + k, device)
            for k, device in enumerate((straight, crossed) if mask else (crossed,))
        ]
        for piece in range(2)
    ]
    ids = [moved(idx, full_idx, 8, straight)] if mask else []
    for copy in away[0] + ids + away[1]:
        copy.start()
    if not mask:
        kept.wait()
    forwards = []
    for piece in range(2):
        for k, copy in enumerate(away[piece]):
            copy.wait_recv()
            here = chunk(full, piece, edge if mask and k == 0 else other)
            forwards.append(moved(here, here, 4 + 2 * piece + k, sibling))
            forwards[-1].start()
        if not mask:
            here = chunk(full, piece, edge)
            forwards.append(moved(here, here, 5 + 2 * piece, sibling))
            forwards[-1].start()
    for copy in away[0] + away[1]:
        copy.wait_send()
    for copy in ids + forwards:
        copy.wait()


def round_kernel(
    other, other_idx, own, here_idx, relations, table, state,
    table_out, state_out, shard_out,
    own_rows, other_rows, rel_kept, factors, grads, pick_own, weights_own, totals, parts, chip_sum, arrived,
    send, recv,
):
    dom, edge = lax.axis_index("dom"), lax.axis_index("edge")
    chip, core = edge // 2, edge % 2
    sibling = (dom, chip * 2 + (1 - core))
    across = (dom, (1 - chip) * 2 + core)
    greet([across, sibling])
    width, rows = own.shape

    def ids_of(b, kind):
        ref = other_idx if b // 2 else here_idx
        return ref[2 * kind + b % 2 : 2 * kind + b % 2 + 1]

    def picked(ids, count):
        row_of = lax.broadcasted_iota(jnp.int32, (count, BLOCK), 0)
        return ones_where(row_of == ids).astype(jnp.bfloat16)

    def own_side(b):
        at = slice(b * BLOCK, (b + 1) * BLOCK)
        chosen = picked(ids_of(b, 0) & 65535, rows)
        pick_own[:, at] = chosen
        m_re, m_im = halves(product(own[...], chosen))
        pick_rel = picked(ids_of(b, 1) & 65535, relations.shape[1])
        rel_re, rel_im = halves(product(relations[...], pick_rel))
        if b // 2:
            rel_im = -rel_im
        rel_kept[:, at] = jnp.concatenate([rel_re, rel_im], axis=0).astype(jnp.bfloat16)
        grads[:, at] = jnp.concatenate(
            [m_re * rel_re - m_im * rel_im, m_re * rel_im + m_im * rel_re], axis=0
        ).astype(jnp.bfloat16)

    def weights(scores, ids, share):
        hits = picked(ids, rows)
        hits = product(hits[:, :LANES] + hits[:, LANES:], jnp.full((LANES, LANES), 1.0, jnp.bfloat16))
        hits = jnp.concatenate([hits, hits], axis=1) * share
        return ((1.0 + jnp.tanh(0.5 * scores)) * hits).astype(jnp.bfloat16)

    def both_sides(b):
        at = slice(b * BLOCK, (b + 1) * BLOCK)
        slot = lax.broadcasted_iota(jnp.int32, (1, BLOCK), 1) + b % 2 * BLOCK
        live = ones_where(slot < ids_of(b, 1) >> 16)
        share = live * (0.5 / rows)
        theirs = product(other[...], picked(ids_of(b, 0) >> 16, rows))
        rel_re, rel_im = halves(rel_kept[:, at].astype(jnp.float32))
        t_re, t_im = halves(theirs)
        u_low = grads[:, at]
        v_low = jnp.concatenate(
            [rel_re * t_re + rel_im * t_im, rel_re * t_im - rel_im * t_re], axis=0
        ).astype(jnp.bfloat16)
        factors[:, at] = v_low
        positive = jnp.sum(u_low.astype(jnp.float32) * theirs, axis=0, keepdims=True)
        weight_pos = -jax.nn.sigmoid(-positive) * live
        negs = ids_of(b, 2)
        w_other = weights(product(other_rows[...], u_low), negs >> 16, share)
        weights_own[:, at] = weights(product(own_rows[...], v_low), negs & 65535, share)
        grad = weight_pos * theirs + product(other[...], w_other)
        g_re, g_im = halves(grad)
        grads[:, at] = jnp.concatenate(
            [g_re * rel_re + g_im * rel_im, g_im * rel_re - g_re * rel_im], axis=0
        ).astype(jnp.bfloat16)

    own_rows[...] = own[...].T
    other_rows[...] = other[...].T
    for b in range(4):
        own_side(b)
        both_sides(b)

    def partial(which, kept):
        at = pl.ds(pl.multiple_of(which * BLOCK, BLOCK), BLOCK)
        total = across_rows(grads[...], pick_own[at, :]) + across_rows(
            factors[...], weights_own[at, :]
        )
        for c in range(2):
            half = total[:, c * LANES : (c + 1) * LANES]
            totals[kept, c] = half
            parts[kept, c] = half.astype(jnp.bfloat16)

    def given(src, at, device):
        return pltpu.make_async_remote_copy(
            src, arrived.at[at], send.at[at], recv.at[at], device_id=device, device_id_type=MESH
        )

    gifts = [
        given(parts.at[0, 1 - core], 0, sibling),
        given(parts.at[1, 1 - core], 1, sibling),
        given(chip_sum, 2, across),
    ]
    partial(1 - chip, 0)
    greeted(2)
    gifts[0].start()
    partial(chip, 1)
    gifts[1].start()
    gifts[0].wait_recv()
    chip_sum[...] = (totals[0, core] + arrived[0].astype(jnp.float32)).astype(jnp.bfloat16)
    gifts[2].start()
    gifts[1].wait_recv()
    grad = totals[1, core] + arrived[1].astype(jnp.float32)
    gifts[2].wait_recv()
    grad = grad + arrived[2].astype(jnp.float32)
    new_state = state[...] + jnp.sum(grad * grad, axis=0, keepdims=True) * (1.0 / width)
    new_table = table[...] - learning_rate * grad / jnp.sqrt(new_state)
    shard_out[...] = new_table.astype(jnp.bfloat16)
    state_out[...] = new_state
    table_out[...] = new_table
    for copy in gifts:
        copy.wait_send()


VMEM = pl.BlockSpec(memory_space=pltpu.VMEM)
DMA = pltpu.SemaphoreType.DMA
LIMIT = 24 * 2**20


def shape(*dims, dtype=jnp.bfloat16):
    return jax.ShapeDtypeStruct(dims, dtype)


def like(array, dtype=None):
    return jax.ShapeDtypeStruct(array.shape, dtype or array.dtype)


def params(collective_id):
    return pltpu.CompilerParams(
        collective_id=collective_id, has_side_effects=True, vmem_limit_bytes=LIMIT
    )


def pack(table, state, ends, rels, negs, counts):
    idx = shape(8, BLOCK, dtype=jnp.int32)
    rest = (ends, rels, negs, counts)
    return pl.pallas_call(
        pack_kernel,
        out_shape=(like(table), like(state), like(table, jnp.bfloat16)) + (idx,) * 4,
        in_specs=[pl.BlockSpec(memory_space=pl.ANY)] * 6,
        out_specs=(VMEM,) * 7,
        scratch_shapes=[pltpu.VMEM(a.shape, a.dtype) for a in rest] + [DMA((6,))],
        compiler_params=pltpu.CompilerParams(vmem_limit_bytes=LIMIT),
        name="pack",
    )(table, state, *rest)


def hand_over_kernel(table, state, table_out, state_out):
    table_out[...] = table[...]
    state_out[...] = state[...]


def hand_over(table, state):
    return pl.pallas_call(
        hand_over_kernel,
        out_shape=(like(table), like(state)),
        in_specs=[VMEM] * 2,
        out_specs=(VMEM,) * 2,
        compiler_params=pltpu.CompilerParams(vmem_limit_bytes=LIMIT),
        name="hand_over",
    )(table, state)


def far(mask, shard, idx):
    return pl.pallas_call(
        functools.partial(far_kernel, mask),
        out_shape=(shape(shard.shape[0], 4 * LANES), like(shard), like(idx)),
        in_specs=[VMEM] * 2,
        out_specs=(VMEM,) * 3,
        scratch_shapes=[DMA((6,)), DMA((6,)), DMA((1,))],
        compiler_params=params(mask),
        name=f"far_{mask}",
    )(shard, idx)


def near(mask, shard, idx):
    return pl.pallas_call(
        functools.partial(near_kernel, mask),
        out_shape=(shape(shard.shape[0], 4 * LANES), like(idx)),
        in_specs=[VMEM] * 2,
        out_specs=(VMEM,) * 2,
        scratch_shapes=[DMA((9,)), DMA((9,)), DMA((1,))],
        compiler_params=params(16 + mask),
        name=f"near_{mask}",
    )(shard, idx)


def one_round(other, other_idx, own, here_idx, relations, table, state):
    width, rows = own.shape
    low, edges = jnp.bfloat16, 4 * BLOCK
    return pl.pallas_call(
        round_kernel,
        out_shape=(like(table), like(state), like(table, low)),
        in_specs=[VMEM] * 7,
        out_specs=(VMEM,) * 3,
        scratch_shapes=[
            pltpu.VMEM((rows, width), low),
            pltpu.VMEM((rows, width), low),
            pltpu.VMEM((width, edges), low),
            pltpu.VMEM((width, edges), low),
            pltpu.VMEM((width, edges), low),
            pltpu.VMEM((rows, edges), low),
            pltpu.VMEM((rows, edges), low),
            pltpu.VMEM((2, 2, width, LANES), jnp.float32),
            pltpu.VMEM((2, 2, width, LANES), low),
            pltpu.VMEM((width, LANES), low),
            pltpu.VMEM((3, width, LANES), low),
            DMA((3,)),
            DMA((3,)),
        ],
        compiler_params=params(24),
        name="one_round",
    )(other, other_idx, own, here_idx, relations, table, state)


def on_device(
    embeddings, adagrad_state, relations, endpoints, relation_ids, negatives, edge_counts, plan
):
    table = embeddings.T
    state = adagrad_state[None, :]
    relations = relations.T
    high, low = plan >> LOW_BITS, plan & (2**LOW_BITS - 1)
    table, state, shard, *packed = pack(
        table, state, endpoints, relation_ids, negatives, edge_counts.reshape(1, -1)
    )
    fars = [functools.partial(far, mask) for mask in range(16)]
    nears = [functools.partial(near, mask) for mask in range(8)]
    for r in range(plan.shape[0]):
        here, away = packed[2 * r : 2 * r + 2]
        own, other, idx = lax.switch(high[r], fars, shard, away)
        other, idx = lax.switch(low[r], nears, other, idx)
        table, state, shard = one_round(other, idx, own, here, relations, table, state)
    table, state = hand_over(table, state)
    return table.T, state[0]


def solution(mesh):
    in_specs = (
        P(("dom", "edge"), None),
        P(("dom", "edge")),
        P(),
        P(None, None, "dom", "edge"),
        P(None, "dom", "edge"),
        P(None, None, "dom", "edge", None),
        P(None, "dom", "edge"),
        P(),
    )
    out_specs = (P(("dom", "edge"), None), P(("dom", "edge")))
    return jax.shard_map(
        on_device, mesh=mesh, in_specs=in_specs, out_specs=out_specs, check_vma=False
    )
```
